512 devices in a mesh: row: 16 (over z, core), col: 32 (over y, x).
Axes of the slice: x: 4, y: 8, z: 8, core: 2. Of those that a mesh axis runs over, the one named last changes fastest.
Arguments:
- eigvecs: float32 [65536, 4096], P('row', 'col'), may hold values from -6 to 6
- reflectors: float32 [2, 65536, 256], P(None, ('row', 'col')), may hold values from -0.046875 to 0.046875
- tau_blocks: float32 [2, 256, 256], replicated, may hold values from -0.375 to 0.375
Outputs:
- transformed: float32 [65536, 4096], P('row', 'col')
The draws below stay inside these ranges and needn't reach their ends.
All inputs are finite; a program needn't handle non-finite values.
Results may differ from the reference program's by a relative error of at most 0.00013.
Values sent between devices are 32-bit elements; how exact they have to be, the bound alone decides.
No kernel may reach another device: no remote copies, remote signals or barrier semaphores. Data moves between devices by JAX's collectives and lax.ppermute only.
A program may use at most 64 MiB of HBM per device.

```python
import jax
import jax.numpy as jnp
from jax import lax

NB = 256
BLOCK = 64
ROWS_DEV = 4096
N_ROWS = 65536
EIGVECS = 4096
N_ROW = 16


def level_of(own_key, extent, shards, least, high):
    def one(dim, shards_of):
        heights = jax.random.uniform(jax.random.fold_in(jax.random.fold_in(own_key, 6), dim), (shards_of,), jnp.float32, least / len(shards), high / len(shards))
        return jnp.repeat(jnp.exp(heights), extent[dim] // shards_of).reshape((-1,) + (1,) * (len(extent) - dim - 1))

    level = one(*shards[0])
    for cut in shards[1:]:
        level = level * one(*cut)
    return level


def centred(own_key, dims, spread, limit, split=(), kind=jnp.bfloat16):
    factor_of = level_of(own_key, dims, split, -0.22, 0.18) if split else 1.0
    values = jax.random.normal(own_key, dims, jnp.float32) * spread * factor_of
    return jnp.minimum(jnp.maximum(values, -limit), limit).astype(kind)


def setup_inputs(seed: int = 0) -> dict:
    seeds = jax.random.split(jax.random.key(seed), 4)
    eigvecs = centred(seeds[0], (N_ROWS, EIGVECS), 1.0, 6.0, ((0, 16), (1, 32)), jnp.float32)
    reflectors = centred(seeds[1], (2, N_ROWS, NB), (N_ROWS // 4) ** -0.5, 0.046875, ((1, 512),), jnp.float32)
    tau_blocks = centred(seeds[2], (2, NB, NB), NB ** -0.5, 0.375, (), jnp.float32)
    return {"eigvecs": eigvecs, "reflectors": reflectors, "tau_blocks": tau_blocks}


def project_on(factor_left, factor_right):
    return jnp.einsum("rk,rc->kc", factor_left, factor_right, precision=lax.Precision.HIGHEST, preferred_element_type=jnp.float32)


def multiply(factor_left, factor_right):
    return jnp.dot(factor_left, factor_right, precision=lax.Precision.HIGHEST, preferred_element_type=jnp.float32)


def reference(eigvecs, reflectors, tau_blocks):
    array_rows = jnp.arange(N_ROWS, dtype=jnp.int32)
    row_owner = array_rows // ROWS_DEV
    local_rows = array_rows % ROWS_DEV
    matrix_rows = (local_rows // BLOCK) * BLOCK * N_ROW + row_owner * BLOCK + local_rows % BLOCK
    matrix_rows = matrix_rows[:, None]
    col_ids = jnp.arange(NB, dtype=jnp.int32)[None, :]
    identity_mat = jnp.eye(NB, dtype=jnp.float32)
    masked_list = []
    triangles = []
    for k in range(2):
        diagonal_at = col_ids + k * NB
        masked_list.append(jnp.where(matrix_rows < diagonal_at, jnp.float32(0.0), jnp.where(matrix_rows == diagonal_at, jnp.float32(1.0), reflectors[k])))
        triangles.append(jnp.triu(tau_blocks[k], 1) + identity_mat)
    w_two = project_on(masked_list[1], eigvecs)
    s_two = multiply(triangles[1], w_two)
    after_two = eigvecs - multiply(masked_list[1], s_two)
    w_one = project_on(masked_list[0], after_two)
    s_one = multiply(triangles[0], w_one)
    return after_two - multiply(masked_list[0], s_one)
```

```python
import jax
import jax.numpy as jnp
from jax import lax
from jax.sharding import PartitionSpec as P

BLOCK = 64


def contract(left, right, left_dim, right_dim, precision=lax.Precision.HIGHEST):
    return lax.dot_general(
        left,
        right,
        (((left_dim,), (right_dim,)), ((), ())),
        precision=precision,
        preferred_element_type=jnp.float32,
    )


def shape_own(drawn, row_index, col_index, row_count):
    panels, rows, width = drawn.shape
    local_rows = col_index * rows + jnp.arange(rows, dtype=jnp.int32)
    matrix_rows = local_rows // BLOCK * BLOCK * row_count + row_index * BLOCK + local_rows % BLOCK
    matrix_rows = matrix_rows[None, :, None]
    diagonal_at = (
        jnp.arange(panels, dtype=jnp.int32)[:, None, None] * width
        + jnp.arange(width, dtype=jnp.int32)[None, None, :]
    )
    return jnp.where(
        matrix_rows < diagonal_at,
        jnp.float32(0.0),
        jnp.where(matrix_rows == diagonal_at, jnp.float32(1.0), drawn),
    )


def sum_everywhere(partial, row_count):
    rows, width = partial.shape
    pieces = partial.reshape(row_count, rows // row_count, width)
    own = jnp.sum(lax.all_to_all(pieces, "row", 0, 0), axis=0)
    own = jnp.sum(lax.all_gather(own, "col"), axis=0)
    return lax.all_gather(own, "row", axis=0, tiled=True)


def shards(eigvecs, reflectors, tau_blocks):
    row_index = lax.axis_index("row")
    col_index = lax.axis_index("col")
    row_count = lax.axis_size("row")
    width = tau_blocks.shape[1]
    identity_mat = jnp.eye(width, dtype=jnp.float32)
    tri_one = jnp.triu(tau_blocks[0], 1) + identity_mat
    tri_two = jnp.triu(tau_blocks[1], 1) + identity_mat

    own = shape_own(reflectors, row_index, col_index, row_count)
    panels = lax.all_gather(own, "col", axis=1, tiled=True)

    gram = sum_everywhere(contract(own[0], own[1], 0, 0), row_count)
    cross = contract(tri_one, contract(gram, tri_two, 1, 0), 1, 0)

    w_two = contract(eigvecs, panels[1], 0, 0, lax.Precision.HIGH)
    w_one = contract(eigvecs, panels[0], 0, 0, lax.Precision.HIGH)
    w_both = jnp.concatenate([w_two, w_one], axis=1)
    pieces = w_both.reshape(row_count, w_both.shape[0] // row_count, 2 * width)
    w_own = jnp.sum(lax.all_to_all(pieces, "row", 0, 0), axis=0)
    s_two = contract(w_own[:, :width], tri_two, 1, 1)
    s_one = contract(w_own[:, width:], tri_one, 1, 1) - contract(w_own[:, :width], cross, 1, 1)
    s_both = lax.all_gather(jnp.concatenate([s_two, s_one], axis=1), "row", axis=0, tiled=True)

    change = contract(panels[1], s_both[:, :width], 1, 1, lax.Precision.HIGH) + contract(
        panels[0], s_both[:, width:], 1, 1, lax.Precision.HIGH
    )
    return eigvecs - change


def solution(mesh):
    in_specs = (P("row", "col"), P(None, ("row", "col"), None), P())
    out_specs = P("row", "col")
    return jax.shard_map(shards, mesh=mesh, in_specs=in_specs, out_specs=out_specs, check_vma=False)
```

```python
import functools

import jax
import jax.numpy as jnp
from jax import lax
from jax.experimental import pallas as pl
from jax.experimental.pallas import tpu as pltpu
from jax.sharding import PartitionSpec as P

BLOCK = 64
NX = 4
NY = 8
ROWS_A = 56
STEP_Y = 2
VMEM = 56 * 1024 * 1024


def split(value):
    high = value.astype(jnp.bfloat16)
    low = (value - high.astype(jnp.float32)).astype(jnp.bfloat16)
    return high, low


def dot(left, right):
    return jnp.dot(left, right, preferred_element_type=jnp.float32)


def shape_own(drawn, row_index, col_index, row_count):
    panels, rows, width = drawn.shape
    local_rows = col_index * rows + jnp.arange(rows, dtype=jnp.int32)
    matrix_rows = local_rows // BLOCK * BLOCK * row_count + row_index * BLOCK + local_rows % BLOCK
    matrix_rows = matrix_rows[None, :, None]
    diagonal_at = (
        jnp.arange(panels, dtype=jnp.int32)[:, None, None] * width
        + jnp.arange(width, dtype=jnp.int32)[None, None, :]
    )
    return jnp.where(
        matrix_rows < diagonal_at,
        jnp.float32(0.0),
        jnp.where(matrix_rows == diagonal_at, jnp.float32(1.0), drawn),
    )


def ring(axis_shift):
    return [(y * NX + x, y * NX + (x + axis_shift) % NX) for y in range(NY) for x in range(NX)]


GROUPS_X = [[y * NX + x for x in range(NX)] for y in range(NY)]
GROUPS_Y = [[y * NX + x for y in range(NY)] for x in range(NX)]


def spread(value, groups):
    count = len(groups[0])
    copies = jnp.broadcast_to(value[None], (count,) + value.shape)
    return lax.all_to_all(copies, "col", 0, 0, axis_index_groups=groups)


def eig_rows(eig_ref, first_y, count_y, x_at):
    parts = []
    for y in range(count_y):
        parts.append(eig_ref[pl.ds((first_y + y) * NX + x_at, 1), ROWS_A:, :])
    block = jnp.concatenate(parts, axis=0)
    return block.reshape(block.shape[0] * block.shape[1], block.shape[2])


def add_products(inner_ref, gram_ref, eig, panel):
    cols = eig.shape[1]
    width = panel.shape[1] // 2
    high, low = split(eig.T)
    parts = jnp.concatenate([high, low], axis=0)
    panel_high, panel_low = split(panel)
    both = dot(parts, panel_high)
    inner_ref[...] += both[:cols] + (both[cols:] + dot(high, panel_low))
    high = panel_high[:, width:].T
    low = panel_low[:, width:].T
    gram_ref[...] += dot(high, panel_high[:, :width]) + (
        dot(low, panel_high[:, :width]) + dot(high, panel_low[:, :width])
    )


def inner_b_kernel(x_ref, eig_ref, own_ref, left_ref, right_ref, inner_ref, gram_ref):
    @pl.when(pl.program_id(0) == 0)
    def _():
        inner_ref[...] = jnp.zeros_like(inner_ref)
        gram_ref[...] = jnp.zeros_like(gram_ref)

    x_at = x_ref[0]
    for panel_ref, shift in ((own_ref, 0), (left_ref, NX - 1), (right_ref, 1)):
        eig = eig_rows(eig_ref, 0, NY // 2, (x_at + shift) % NX)
        add_products(inner_ref, gram_ref, eig, panel_ref[...])


def inner_b(x_at, eig_blocks, own, left, right):
    blocks, block_rows, cols = eig_blocks.shape
    rows, width = own.shape
    piece = pl.BlockSpec((rows // 2, width), lambda i, x: (i, 0))
    shapes = [(cols, width), (width // 2, width // 2)]
    return pl.pallas_call(
        inner_b_kernel,
        grid_spec=pltpu.PrefetchScalarGridSpec(
            num_scalar_prefetch=1,
            grid=(2,),
            in_specs=[pl.BlockSpec((blocks // 2, block_rows, cols), lambda i, x: (i, 0, 0)), piece, piece, piece],
            out_specs=[pl.BlockSpec(shape, lambda i, x: (0, 0)) for shape in shapes],
        ),
        out_shape=[jax.ShapeDtypeStruct(shape, jnp.float32) for shape in shapes],
        compiler_params=pltpu.CompilerParams(vmem_limit_bytes=VMEM),
        cost_estimate=pl.CostEstimate(
            flops=36 * rows * cols * width, bytes_accessed=16 * rows * width, transcendentals=0
        ),
    )(x_at, eig_blocks, own, left, right)


def inner_a_kernel(
    x_ref, eig_ref, far_eig_ref, panel_ref, far_low_ref, far_high_ref, inner_start, gram_start, out_ref, inner_ref, gram_ref
):
    step = pl.program_id(0)
    x_far = (x_ref[0] + NX // 2) % NX

    @pl.when(step == 0)
    def _():
        inner_ref[...] = inner_start[...]
        gram_ref[...] = gram_start[...]
        add_products(inner_ref, gram_ref, eig_rows(far_eig_ref, 0, NY // 2, x_far), far_low_ref[...])

    @pl.when(step == 1)
    def _():
        add_products(inner_ref, gram_ref, eig_rows(far_eig_ref, 0, NY // 2, x_far), far_high_ref[...])

    eig = eig_ref[:, :ROWS_A, :]
    add_products(inner_ref, gram_ref, eig.reshape(eig.shape[0] * ROWS_A, eig.shape[2]), panel_ref[...])

    @pl.when(step == pl.num_programs(0) - 1)
    def _():
        shares, share, width = out_ref.shape
        half = gram_ref.shape[0] // 2
        out_ref[:, : share // 2, :] = inner_ref[...].reshape(shares, share // 2, width)
        gram = jnp.concatenate([gram_ref[:half, :], gram_ref[half:, :]], axis=1)
        out_ref[:, share // 2 :, :] = gram.reshape(shares, share // 2, width)


def inner_a(shares, x_at, eig_blocks, panels, far_low, far_high, inner, gram):
    blocks, block_rows, cols = eig_blocks.shape
    rows, width = panels.shape
    steps = NY // STEP_Y
    whole = lambda value: pl.BlockSpec(value.shape, lambda i, x: (0, 0))
    shape = (shares, 2 * cols // shares, width)
    return pl.pallas_call(
        inner_a_kernel,
        grid_spec=pltpu.PrefetchScalarGridSpec(
            num_scalar_prefetch=1,
            grid=(steps,),
            in_specs=[
                pl.BlockSpec((blocks // steps, block_rows, cols), lambda i, x: (i, 0, 0)),
                pl.BlockSpec((blocks // 2, block_rows, cols), lambda i, x: (jnp.minimum(i, 1), 0, 0)),
                pl.BlockSpec((rows // steps, width), lambda i, x: (i, 0)),
                whole(far_low),
                whole(far_high),
                whole(inner),
                whole(gram),
            ],
            out_specs=pl.BlockSpec(shape, lambda i, x: (0, 0, 0)),
            scratch_shapes=[pltpu.VMEM(inner.shape, jnp.float32), pltpu.VMEM(gram.shape, jnp.float32)],
        ),
        out_shape=jax.ShapeDtypeStruct(shape, jnp.float32),
        compiler_params=pltpu.CompilerParams(vmem_limit_bytes=VMEM),
        cost_estimate=pl.CostEstimate(
            flops=14 * rows * cols * width, bytes_accessed=5 * rows * width, transcendentals=0
        ),
    )(x_at, eig_blocks, eig_blocks, panels, far_low, far_high, inner, gram)


def times(left, right):
    return lax.dot_general(
        left,
        right,
        (((1,), (1,)), ((), ())),
        precision=lax.Precision.HIGHEST,
        preferred_element_type=jnp.float32,
    )


def triangle(tau):
    row = lax.broadcasted_iota(jnp.int32, tau.shape, 0)
    col = lax.broadcasted_iota(jnp.int32, tau.shape, 1)
    return jnp.where(row < col, tau, jnp.where(row == col, jnp.float32(1.0), jnp.float32(0.0)))


def update_kernel(
    x_ref, eig_ref, sums_ref, tau_ref, panel_ref, own_ref, left_ref, right_ref, far_low_ref, far_high_ref, out_ref, parts_ref
):
    cols = eig_ref.shape[2]
    width = tau_ref.shape[1]
    step = pl.program_id(0)
    half = pl.num_programs(0) // 2
    x_at = x_ref[0]

    @pl.when(step == 0)
    def _():
        own_cols = sums_ref.shape[1] // 2
        inner = sums_ref[:, :own_cols, :].reshape(cols, 2 * width)
        gram = sums_ref[:, own_cols:, :].reshape(cols, 2 * width)
        gram = jnp.concatenate([gram[:, :width], gram[:, width:]], axis=0)
        s_two = times(inner[:, :width], triangle(tau_ref[1]))
        s_one = times(inner[:, width:] - times(s_two, gram), triangle(tau_ref[0]))
        high, low = split(jnp.concatenate([s_two, s_one], axis=1).T)
        parts_ref[:, :cols] = high
        parts_ref[:, cols:] = low

    def change(panel):
        high, low = split(panel)
        both = dot(high, parts_ref[...])
        return both[:, :cols] + (both[:, cols:] + dot(low, parts_ref[:, :cols]))

    panel = panel_ref[...]
    blocks = eig_ref.shape[0]
    out_ref[:, :ROWS_A, :] = eig_ref[:, :ROWS_A, :] - change(panel).reshape(blocks, ROWS_A, cols)

    def update_rest(panel, shift):
        part = change(panel).reshape(STEP_Y, -1, cols)
        x_from = (x_at + shift) % NX
        for y in range(STEP_Y):
            at = pl.ds(y * NX + x_from, 1)
            out_ref[at, ROWS_A:, :] = eig_ref[at, ROWS_A:, :] - part[y : y + 1]

    update_rest(own_ref[...], 0)
    update_rest(left_ref[...], NX - 1)
    update_rest(right_ref[...], 1)
    update_rest(jnp.where(step < half, far_low_ref[...], far_high_ref[...]), NX // 2)


def update(x_at, eig_blocks, sums, tau, panels, own, left, right, far_low, far_high):
    blocks, block_rows, cols = eig_blocks.shape
    rows, width = panels.shape
    steps = NY // STEP_Y
    half = steps // 2
    piece_rows = own.shape[0] // steps
    piece = pl.BlockSpec((piece_rows, width), lambda i, x: (i, 0))
    block = pl.BlockSpec((blocks // steps, block_rows, cols), lambda i, x: (i, 0, 0))
    return pl.pallas_call(
        update_kernel,
        grid_spec=pltpu.PrefetchScalarGridSpec(
            num_scalar_prefetch=1,
            grid=(steps,),
            in_specs=[
                block,
                pl.BlockSpec(sums.shape, lambda i, x: (0, 0, 0)),
                pl.BlockSpec(tau.shape, lambda i, x: (0, 0, 0)),
                pl.BlockSpec((rows // steps, width), lambda i, x: (i, 0)),
                piece,
                piece,
                piece,
                pl.BlockSpec((piece_rows, width), lambda i, x: (jnp.minimum(i, half - 1), 0)),
                pl.BlockSpec((piece_rows, width), lambda i, x: (jnp.maximum(i - half, 0), 0)),
            ],
            out_specs=block,
            scratch_shapes=[pltpu.VMEM((width, 2 * cols), jnp.bfloat16)],
        ),
        out_shape=jax.ShapeDtypeStruct(eig_blocks.shape, jnp.float32),
        compiler_params=pltpu.CompilerParams(vmem_limit_bytes=VMEM),
        cost_estimate=pl.CostEstimate(
            flops=6 * blocks * block_rows * cols * width,
            bytes_accessed=4 * blocks * block_rows * (width + 2 * cols),
            transcendentals=0,
        ),
    )(x_at, eig_blocks, sums, tau, panels, own, left, right, far_low, far_high)


def shards(eigvecs, reflectors, tau_blocks):
    row_index = lax.axis_index("row")
    col_index = lax.axis_index("col")
    row_count = lax.axis_size("row")
    col_count = lax.axis_size("col")
    width = tau_blocks.shape[1]
    cols = eigvecs.shape[1]
    x_at = (col_index % NX).astype(jnp.int32)[None]
    eig_blocks = eigvecs.reshape(col_count, eigvecs.shape[0] // col_count, cols)

    own_panels = shape_own(reflectors, row_index, col_index, row_count)
    own = jnp.concatenate([own_panels[1], own_panels[0]], axis=1)

    part_a = lax.all_gather(own[:ROWS_A], "col", axis=0, tiled=True, axis_index_groups=GROUPS_X)
    part_b = spread(own[ROWS_A:], GROUPS_Y).reshape(-1, 2 * width)
    part_a, part_b = lax.optimization_barrier((part_a, part_b))
    panels_a = lax.all_gather(part_a, "col", axis=0, tiled=True, axis_index_groups=GROUPS_Y)
    left = lax.ppermute(part_b, "col", ring(1))
    right = lax.ppermute(part_b, "col", ring(-1))
    half = part_b.shape[0] // 2
    far_low = lax.ppermute(left[:half], "col", ring(1))
    far_high = lax.ppermute(right[half:], "col", ring(-1))

    inner, gram = inner_b(x_at, eig_blocks, part_b, left, right)
    shares = inner_a(row_count, x_at, eig_blocks, panels_a, far_low, far_high, inner, gram)
    share = jnp.sum(lax.all_to_all(shares, "row", 0, 0), axis=0)
    sums = lax.all_gather(share, "row")
    out = update(x_at, eig_blocks, sums, tau_blocks, panels_a, part_b, left, right, far_low, far_high)
    return out.reshape(eigvecs.shape)


def solution(mesh):
    in_specs = (P("row", "col"), P(None, ("row", "col"), None), P())
    out_specs = P("row", "col")
    return jax.shard_map(shards, mesh=mesh, in_specs=in_specs, out_specs=out_specs, check_vma=False)
```

```python
import functools

import jax
import jax.numpy as jnp
from jax import lax
from jax.experimental import pallas as pl
from jax.experimental.pallas import tpu as pltpu
from jax.sharding import PartitionSpec as P

BLOCK = 64
NX = 4
NY = 8
VMEM = 60 * 1024 * 1024


def split(value):
    high = value.astype(jnp.bfloat16)
    low = (value - high.astype(jnp.float32)).astype(jnp.bfloat16)
    return high, low


def dot(left, right):
    return jnp.dot(left, right, preferred_element_type=jnp.float32)


def shape_own(drawn, row_index, col_index, row_count):
    panels, rows, width = drawn.shape
    local_rows = col_index * rows + jnp.arange(rows, dtype=jnp.int32)
    matrix_rows = local_rows // BLOCK * BLOCK * row_count + row_index * BLOCK + local_rows % BLOCK
    matrix_rows = matrix_rows[None, :, None]
    diagonal_at = (
        jnp.arange(panels, dtype=jnp.int32)[:, None, None] * width
        + jnp.arange(width, dtype=jnp.int32)[None, None, :]
    )
    return jnp.where(
        matrix_rows < diagonal_at,
        jnp.float32(0.0),
        jnp.where(matrix_rows == diagonal_at, jnp.float32(1.0), drawn),
    )


def move_x(value, shift):
    pairs = [(y * NX + x, y * NX + (x + shift) % NX) for y in range(NY) for x in range(NX)]
    return lax.ppermute(value, "col", pairs)


def move_y(value, shift):
    pairs = [(y * NX + x, (y + shift) % NY * NX + x) for y in range(NY) for x in range(NX)]
    return lax.ppermute(value, "col", pairs)


GROUPS_X = [[y * NX + x for x in range(NX)] for y in range(NY)]
GROUPS_Y = [[y * NX + x for y in range(NY)] for x in range(NX)]


def spread(value, groups):
    count = len(groups[0])
    copies = jnp.broadcast_to(value[None], (count,) + value.shape)
    return lax.all_to_all(copies, "col", 0, 0, axis_index_groups=groups)


OWN = [("a", 0, 0, NX), ("b", 0, 0, NY)]
NEAR = [("a", -1, 0, NX), ("a", 1, 0, NX), ("a", -2, 0, NX), ("a", 2, 0, NX), ("b", -1, 0, NY), ("b", 1, 0, NY)]
FAR = [("a", -3, 0, NX), ("a", 3, 0, NX), ("b", NX // 2, 0, NY), ("a", NY // 2, 0, NX)]


def place(piece, at):
    kind, shift, first, _ = piece
    if kind == "a":
        return (at[0] + shift + NY) % NY, first
    return first, (at[1] + shift + NX) % NX


def block_shape(piece):
    kind, _, _, count = piece
    return (1, count) if kind == "a" else (count, 1)


def add_products(inner_ref, gram_ref, eig, panel):
    cols = eig.shape[1]
    width = panel.shape[1] // 2
    high, low = split(eig.T)
    parts = jnp.concatenate([high, low], axis=0)
    panel_high, panel_low = split(panel)
    both = dot(parts, panel_high)
    inner_ref[...] += both[:cols] + (both[cols:] + dot(high, panel_low))
    high = panel_high[:, width:].T
    low = panel_low[:, width:].T
    gram_ref[...] += dot(high, panel_high[:, :width]) + (
        dot(low, panel_high[:, :width]) + dot(high, panel_low[:, :width])
    )


def inner_kernel(count, first, last, at_ref, *refs):
    eigs, panels, refs = refs[:count], refs[count : 2 * count], refs[2 * count :]
    if first:
        starts = None
    else:
        starts, refs = refs[:2], refs[2:]
    outs, (inner_ref, gram_ref) = refs[:-2], refs[-2:]
    inner_ref[...] = jnp.zeros_like(inner_ref) if first else starts[0][...]
    gram_ref[...] = jnp.zeros_like(gram_ref) if first else starts[1][...]
    for eig_ref, panel_ref in zip(eigs, panels):
        add_products(inner_ref, gram_ref, eig_ref[...].reshape(panel_ref.shape[0], -1), panel_ref[...])
    if not last:
        outs[0][...] = inner_ref[...]
        outs[1][...] = gram_ref[...]
        return
    (out_ref,) = outs
    shares, share, width = out_ref.shape
    half = gram_ref.shape[0] // 2
    out_ref[:, : share // 2, :] = inner_ref[...].reshape(shares, share // 2, width)
    gram = jnp.concatenate([gram_ref[:half, :], gram_ref[half:, :]], axis=1)
    out_ref[:, share // 2 :, :] = gram.reshape(shares, share // 2, width)


def inner_products(at, eigs, pieces, panels, starts, shares):
    _, _, _, rows, cols = eigs.shape
    width = panels[0].shape[1]
    total = sum(panel.shape[0] for panel in panels)
    state = [(cols, width), (width // 2, width // 2)]
    outs = [(shares, 2 * cols // shares, width)] if shares else state

    def eig_spec(piece):
        half = 0 if piece[0] == "a" else 1
        shape = block_shape(piece)

        def index(i, at_ref):
            y, x = place(piece, (at_ref[0], at_ref[1]))
            return y // shape[0], x // shape[1], half, 0, 0

        return pl.BlockSpec(shape + (1, rows, cols), index)

    def whole(shape):
        return pl.BlockSpec(shape, lambda i, at_ref: (0,) * len(shape))

    return pl.pallas_call(
        functools.partial(inner_kernel, len(pieces), starts is None, bool(shares)),
        grid_spec=pltpu.PrefetchScalarGridSpec(
            num_scalar_prefetch=1,
            grid=(1,),
            in_specs=[eig_spec(piece) for piece in pieces]
            + [whole(panel.shape) for panel in panels]
            + ([] if starts is None else [whole(shape) for shape in state]),
            out_specs=[whole(shape) for shape in outs],
            scratch_shapes=[pltpu.VMEM(shape, jnp.float32) for shape in state],
        ),
        out_shape=[jax.ShapeDtypeStruct(shape, jnp.float32) for shape in outs],
        compiler_params=pltpu.CompilerParams(vmem_limit_bytes=VMEM),
        cost_estimate=pl.CostEstimate(
            flops=12 * total * cols * width, bytes_accessed=4 * total * (width + cols), transcendentals=0
        ),
    )(at, *[eigs] * len(pieces), *panels, *([] if starts is None else starts))


def times(left, right):
    return lax.dot_general(
        left,
        right,
        (((1,), (1,)), ((), ())),
        precision=lax.Precision.HIGHEST,
        preferred_element_type=jnp.float32,
    )


def triangle(tau):
    row = lax.broadcasted_iota(jnp.int32, tau.shape, 0)
    col = lax.broadcasted_iota(jnp.int32, tau.shape, 1)
    return jnp.where(row < col, tau, jnp.where(row == col, jnp.float32(1.0), jnp.float32(0.0)))


def update_kernel(pieces, at_ref, sums_ref, tau_ref, eig_ref, *refs):
    count = len(pieces)
    panels, out_ref = refs[:count], refs[count]
    parts_ref, panel_buf, eig_buf, panel_sems, eig_sems, out_sems = refs[count + 1 :]
    rows, cols = eig_ref.shape[3:]
    width = tau_ref.shape[1]

    loads, stores, spans, first = [], [], [], 0
    for n, piece in enumerate(pieces):
        size = panels[n].shape[0]
        y, x = place(piece, (at_ref[0], at_ref[1]))
        shape = block_shape(piece)
        at = (pl.ds(y, shape[0]), pl.ds(x, shape[1]), 0 if piece[0] == "a" else 1)
        span = pl.ds(first // rows, size // rows)
        local = eig_buf.at[span].reshape(shape + (rows, cols))
        loads.append(
            (
                pltpu.make_async_copy(panels[n], panel_buf.at[pl.ds(first, size)], panel_sems.at[n]),
                pltpu.make_async_copy(eig_ref.at[at], local, eig_sems.at[n]),
            )
        )
        stores.append(pltpu.make_async_copy(local, out_ref.at[at], out_sems.at[n]))
        spans.append((first, size))
        first += size
    for load in loads:
        for copy in load:
            copy.start()

    own_cols = sums_ref.shape[1] // 2
    inner = sums_ref[:, :own_cols, :].reshape(cols, 2 * width)
    gram = sums_ref[:, own_cols:, :].reshape(cols, 2 * width)
    gram = jnp.concatenate([gram[:, :width], gram[:, width:]], axis=0)
    s_two = times(inner[:, :width], triangle(tau_ref[1]))
    s_one = times(inner[:, width:] - times(s_two, gram), triangle(tau_ref[0]))
    high, low = split(jnp.concatenate([s_two, s_one], axis=1).T)
    parts_ref[:, :cols] = high
    parts_ref[:, cols:] = low

    for load, store, (first, size) in zip(loads, stores, spans):
        for copy in load:
            copy.wait()
        high, low = split(panel_buf[first : first + size, :])
        both = dot(high, parts_ref[...])
        change = both[:, :cols] + (both[:, cols:] + dot(low, parts_ref[:, :cols]))
        span = slice(first // rows, (first + size) // rows)
        eig_buf[span] = eig_buf[span] - change.reshape(size // rows, rows, cols)
        store.start()
    for store in stores:
        store.wait()


def update(at, eigs, sums, tau, pieces, panels):
    rows, cols = eigs.shape[3:]
    width = panels[0].shape[1]
    total = sum(panel.shape[0] for panel in panels)
    anywhere = pl.BlockSpec(memory_space=pl.ANY)
    return pl.pallas_call(
        functools.partial(update_kernel, pieces),
        grid_spec=pltpu.PrefetchScalarGridSpec(
            num_scalar_prefetch=1,
            grid=(1,),
            in_specs=[
                pl.BlockSpec(sums.shape, lambda i, at_ref: (0, 0, 0)),
                pl.BlockSpec(tau.shape, lambda i, at_ref: (0, 0, 0)),
                anywhere,
            ]
            + [anywhere] * len(panels),
            out_specs=anywhere,
            scratch_shapes=[
                pltpu.VMEM((width, 2 * cols), jnp.bfloat16),
                pltpu.VMEM((total, width), jnp.float32),
                pltpu.VMEM((total // rows, rows, cols), jnp.float32),
            ]
            + [pltpu.SemaphoreType.DMA((len(pieces),))] * 3,
        ),
        out_shape=jax.ShapeDtypeStruct(eigs.shape, jnp.float32),
        compiler_params=pltpu.CompilerParams(vmem_limit_bytes=VMEM),
        cost_estimate=pl.CostEstimate(
            flops=6 * total * cols * width, bytes_accessed=4 * total * (width + 2 * cols), transcendentals=0
        ),
    )(at, sums, tau, eigs, *panels)


def shards(eigvecs, reflectors, tau_blocks):
    row_index = lax.axis_index("row")
    col_index = lax.axis_index("col")
    row_count = lax.axis_size("row")
    cols = eigvecs.shape[1]
    width = 2 * tau_blocks.shape[1]
    half = reflectors.shape[1] // 2
    at = jnp.stack([col_index // NX, col_index % NX]).astype(jnp.int32)
    eigs = eigvecs.reshape(NY, NX, 2, half, cols)

    own = shape_own(reflectors, row_index, col_index, row_count)
    own = jnp.concatenate([own[1], own[0]], axis=1)

    own_a = lax.all_gather(own[:half], "col", axis=0, tiled=True, axis_index_groups=GROUPS_X)
    own_b = spread(own[half:], GROUPS_Y).reshape(-1, width)
    own_b, _ = lax.optimization_barrier((own_b, own_a))
    up, down = [own_a], [own_a]
    for _ in range(NY // 2 - 1):
        up.append(move_y(up[-1], 1))
        down.append(move_y(down[-1], -1))
    left, right = move_x(own_b, 1), move_x(own_b, -1)
    far_b = move_x(left, 1)
    far_a = move_y(up[-1], 1)

    near = [up[1], down[1], up[2], down[2], left, right]
    far = [up[3], down[3], far_b, far_a]
    state = inner_products(at, eigs, OWN, [own_a, own_b], None, 0)
    state = inner_products(at, eigs, NEAR, near, state, 0)
    (shares,) = inner_products(at, eigs, FAR, far, state, row_count)
    share = jnp.sum(lax.all_to_all(shares, "row", 0, 0), axis=0)
    sums = lax.all_gather(share, "row")

    out = update(at, eigs, sums, tau_blocks, OWN + NEAR + FAR, [own_a, own_b] + near + far)
    return out.reshape(eigvecs.shape)


def solution(mesh):
    in_specs = (P("row", "col"), P(None, ("row", "col"), None), P())
    out_specs = P("row", "col")
    return jax.shard_map(shards, mesh=mesh, in_specs=in_specs, out_specs=out_specs, check_vma=False)
```

```python
import functools

import jax
import jax.numpy as jnp
from jax import lax
from jax.experimental import pallas as pl
from jax.experimental.pallas import tpu as pltpu
from jax.sharding import PartitionSpec as P

BLOCK = 64
NX = 4
NY = 8
AHEAD = 4
ROWS_A = 64
VMEM_INNER = 16 * 1024 * 1024
VMEM_UPDATE = 24 * 1024 * 1024


def split(value):
    high = value.astype(jnp.bfloat16)
    low = (value - high.astype(jnp.float32)).astype(jnp.bfloat16)
    return high, low


def dot(left, right):
    return jnp.dot(left, right, preferred_element_type=jnp.float32)


def shape_own(drawn, row_index, col_index, row_count):
    panels, rows, width = drawn.shape
    local_rows = col_index * rows + jnp.arange(rows, dtype=jnp.int32)
    matrix_rows = local_rows // BLOCK * BLOCK * row_count + row_index * BLOCK + local_rows % BLOCK
    matrix_rows = matrix_rows[None, :, None]
    diagonal_at = (
        jnp.arange(panels, dtype=jnp.int32)[:, None, None] * width
        + jnp.arange(width, dtype=jnp.int32)[None, None, :]
    )
    return jnp.where(
        matrix_rows < diagonal_at,
        jnp.float32(0.0),
        jnp.where(matrix_rows == diagonal_at, jnp.float32(1.0), drawn),
    )


def move_x(value, shift):
    pairs = [(y * NX + x, y * NX + (x + shift) % NX) for y in range(NY) for x in range(NX)]
    return lax.ppermute(value, "col", pairs)


def move_y(value, shift):
    pairs = [(y * NX + x, (y + shift) % NY * NX + x) for y in range(NY) for x in range(NX)]
    return lax.ppermute(value, "col", pairs)


GROUPS_X = [[y * NX + x for x in range(NX)] for y in range(NY)]
GROUPS_Y = [[y * NX + x for y in range(NY)] for x in range(NX)]


def spread(value, groups):
    count = len(groups[0])
    copies = jnp.broadcast_to(value[None], (count,) + value.shape)
    return lax.all_to_all(copies, "col", 0, 0, axis_index_groups=groups)


SHIFTS_B = [0, -1, 1, NX // 2]
SHIFTS_A = [0, -1, 1, -2, 2, -3, 3, NY // 2]


def eig_a(y):
    return pl.ds(y, 1), pl.ds(0, NX), pl.ds(0, ROWS_A)


def eig_b(x, rows):
    return pl.ds(0, NY), pl.ds(x, 1), pl.ds(ROWS_A, rows - ROWS_A)


def pieces_of(at_ref, shifts, rows):
    places = [eig_b(at_ref[SHIFTS_B.index(shift)], rows) for shift in shifts[0]]
    return places + [eig_a(at_ref[NX + SHIFTS_A.index(shift)]) for shift in shifts[1]]


def load(source, target, sem):
    copy = pltpu.make_async_copy(source, target, sem)
    copy.start()
    return copy


def add_products(inner_ref, gram_ref, eig, panel):
    cols = eig.shape[1]
    width = panel.shape[1] // 2
    high, low = split(eig.T)
    parts = jnp.concatenate([high, low], axis=0)
    panel_high, panel_low = split(panel)
    both = dot(parts, panel_high)
    inner_ref[...] += both[:cols] + (both[cols:] + dot(high, panel_low))
    high = panel_high[:, width:].T
    low = panel_low[:, width:].T
    gram_ref[...] += dot(high, panel_high[:, :width]) + (
        dot(low, panel_high[:, :width]) + dot(high, panel_low[:, :width])
    )


def whole(value):
    return pl.BlockSpec(value.shape, lambda i, at_ref: (0,) * len(value.shape))


def inner_kernel(shifts, first, last, at_ref, eig_ref, *refs):
    count = len(shifts[0]) + len(shifts[1])
    panels, refs = refs[:count], refs[count:]
    if first:
        starts = None
    else:
        starts, refs = refs[:2], refs[2:]
    outs, (inner_ref, gram_ref) = refs[:-2], refs[-2:]
    inner_ref[...] = jnp.zeros_like(inner_ref) if first else starts[0][...]
    gram_ref[...] = jnp.zeros_like(gram_ref) if first else starts[1][...]
    for panel_ref, where in zip(panels, pieces_of(at_ref, shifts, eig_ref.shape[2])):
        eig = eig_ref[where]
        add_products(inner_ref, gram_ref, eig.reshape(-1, eig.shape[-1]), panel_ref[...])
    if not last:
        outs[0][...] = inner_ref[...]
        outs[1][...] = gram_ref[...]
        return
    (out_ref,) = outs
    shares, share, width = out_ref.shape
    half = gram_ref.shape[0] // 2
    out_ref[:, : share // 2, :] = inner_ref[...].reshape(shares, share // 2, width)
    gram = jnp.concatenate([gram_ref[:half, :], gram_ref[half:, :]], axis=1)
    out_ref[:, share // 2 :, :] = gram.reshape(shares, share // 2, width)


def inner_products(at, eigs, shifts, panels, starts, shares):
    cols = eigs.shape[3]
    width = panels[0].shape[1]
    total = sum(panel.shape[0] for panel in panels)
    state = [jax.ShapeDtypeStruct(shape, jnp.float32) for shape in [(cols, width), (width // 2, width // 2)]]
    outs = [jax.ShapeDtypeStruct((shares, 2 * cols // shares, width), jnp.float32)] if shares else state
    args = [eigs, *panels] + ([] if starts is None else list(starts))
    return pl.pallas_call(
        functools.partial(inner_kernel, shifts, starts is None, bool(shares)),
        grid_spec=pltpu.PrefetchScalarGridSpec(
            num_scalar_prefetch=1,
            grid=(1,),
            in_specs=[whole(arg) for arg in args],
            out_specs=[whole(out) for out in outs],
            scratch_shapes=[pltpu.VMEM(shape.shape, jnp.float32) for shape in state],
        ),
        out_shape=outs,
        compiler_params=pltpu.CompilerParams(vmem_limit_bytes=VMEM_INNER),
        cost_estimate=pl.CostEstimate(
            flops=12 * total * cols * width, bytes_accessed=4 * total * (width + cols), transcendentals=0
        ),
    )(at, *args)


def times(left, right):
    return lax.dot_general(
        left,
        right,
        (((1,), (1,)), ((), ())),
        precision=lax.Precision.HIGHEST,
        preferred_element_type=jnp.float32,
    )


def triangle(tau):
    row = lax.broadcasted_iota(jnp.int32, tau.shape, 0)
    col = lax.broadcasted_iota(jnp.int32, tau.shape, 1)
    return jnp.where(row < col, tau, jnp.where(row == col, jnp.float32(1.0), jnp.float32(0.0)))


def update_kernel(at_ref, sums_ref, tau_hbm, eig_hbm, *refs):
    panels, out_ref = refs[: NX + NY], refs[NX + NY]
    parts_ref, tau_ref, eig_ref, buf_ref, own_sems, sems, out_sems = refs[NX + NY + 1 :]
    rows, cols = eig_ref.shape[2:]
    width = tau_ref.shape[1]
    tau_load = load(tau_hbm, tau_ref, own_sems.at[0])
    eig_load = load(eig_hbm, eig_ref, own_sems.at[1])
    spans = [0]
    for panel_ref in panels:
        spans.append(spans[-1] + panel_ref.shape[0])

    def start(n):
        return load(panels[n], buf_ref.at[pl.ds(spans[n], panels[n].shape[0])], sems.at[n])

    copies = [start(n) for n in range(AHEAD)]
    tau_load.wait()
    own_cols = sums_ref.shape[1] // 2
    inner = sums_ref[:, :own_cols, :].reshape(cols, 2 * width)
    gram = sums_ref[:, own_cols:, :].reshape(cols, 2 * width)
    gram = jnp.concatenate([gram[:, :width], gram[:, width:]], axis=0)
    s_two = times(inner[:, :width], triangle(tau_ref[1]))
    s_one = times(inner[:, width:] - times(s_two, gram), triangle(tau_ref[0]))
    high, low = split(jnp.concatenate([s_two, s_one], axis=1).T)
    parts_ref[:, :cols] = high
    parts_ref[:, cols:] = low

    eig_load.wait()
    stores = []
    for n, where in enumerate(pieces_of(at_ref, (SHIFTS_B, SHIFTS_A), rows)):
        copies[n].wait()
        if n + AHEAD < len(panels):
            copies.append(start(n + AHEAD))
        high, low = split(buf_ref[spans[n] : spans[n + 1], :])
        both = dot(high, parts_ref[...])
        change = both[:, :cols] + (both[:, cols:] + dot(low, parts_ref[:, :cols]))
        old = eig_ref[where]
        eig_ref[where] = old - change.reshape(old.shape)
        if n >= NX:
            stores.append(load(eig_ref.at[where[0]], out_ref.at[where[0]], out_sems.at[n - NX]))
    for copy in stores:
        copy.wait()


def in_hbm(value):
    return pltpu.with_memory_space_constraint(value, pltpu.HBM)


def update(at, eigs, sums, tau, panels):
    cols = eigs.shape[3]
    width = panels[0].shape[1]
    total = sum(panel.shape[0] for panel in panels)
    anywhere = pl.BlockSpec(memory_space=pl.ANY)
    return pl.pallas_call(
        update_kernel,
        grid_spec=pltpu.PrefetchScalarGridSpec(
            num_scalar_prefetch=1,
            grid=(1,),
            in_specs=[whole(sums)] + [anywhere] * (2 + len(panels)),
            out_specs=anywhere,
            scratch_shapes=[
                pltpu.VMEM((width, 2 * cols), jnp.bfloat16),
                pltpu.VMEM(tau.shape, jnp.float32),
                pltpu.VMEM(eigs.shape, jnp.float32),
                pltpu.VMEM((total, width), jnp.float32),
                pltpu.SemaphoreType.DMA((2,)),
                pltpu.SemaphoreType.DMA((NX + NY,)),
                pltpu.SemaphoreType.DMA((NY,)),
            ],
        ),
        out_shape=jax.ShapeDtypeStruct(eigs.shape, jnp.float32),
        compiler_params=pltpu.CompilerParams(vmem_limit_bytes=VMEM_UPDATE),
        cost_estimate=pl.CostEstimate(
            flops=6 * total * cols * width, bytes_accessed=4 * total * (width + 2 * cols), transcendentals=0
        ),
    )(at, sums, in_hbm(tau), in_hbm(eigs), *[in_hbm(panel) for panel in panels])


def shards(eigvecs, reflectors, tau_blocks):
    row_index = lax.axis_index("row")
    col_index = lax.axis_index("col")
    row_count = lax.axis_size("row")
    width = 2 * tau_blocks.shape[1]
    y_at, x_at = (col_index // NX).astype(jnp.int32), (col_index % NX).astype(jnp.int32)
    at = jnp.concatenate(
        [(x_at + NX + jnp.array(SHIFTS_B, jnp.int32)) % NX, (y_at + NY + jnp.array(SHIFTS_A, jnp.int32)) % NY]
    )
    eigs = eigvecs.reshape(NY, NX, reflectors.shape[1], eigvecs.shape[1])

    own = shape_own(reflectors, row_index, col_index, row_count)
    own = jnp.concatenate([own[1], own[0]], axis=1)

    own_a = lax.all_gather(own[:ROWS_A], "col", axis=0, tiled=True, axis_index_groups=GROUPS_X)
    own_b = spread(own[ROWS_A:], GROUPS_Y).reshape(-1, width)
    own_b, _ = lax.optimization_barrier((own_b, own_a))
    up, down = [own_a], [own_a]
    for _ in range(NY // 2 - 1):
        up.append(move_y(up[-1], 1))
        down.append(move_y(down[-1], -1))
    far_a = move_y(up[-1], 1)
    left, right = move_x(own_b, 1), move_x(own_b, -1)
    far_b = move_x(left, 1)

    state = inner_products(at, eigs, ([0], [0, -1, 1]), [own_b, own_a, up[1], down[1]], None, 0)
    state = inner_products(at, eigs, ([-1, 1], [-2, 2]), [left, right, up[2], down[2]], state, 0)
    (shares,) = inner_products(
        at, eigs, ([NX // 2], [-3, 3, NY // 2]), [far_b, up[3], down[3], far_a], state, row_count
    )
    share = jnp.sum(lax.all_to_all(shares, "row", 0, 0), axis=0)
    sums = lax.all_gather(share, "row")

    panels = [own_b, left, right, far_b, own_a, up[1], down[1], up[2], down[2], up[3], down[3], far_a]
    return update(at, eigs, sums, tau_blocks, panels).reshape(eigvecs.shape)


def solution(mesh):
    in_specs = (P("row", "col"), P(None, ("row", "col"), None), P())
    out_specs = P("row", "col")
    return jax.shard_map(shards, mesh=mesh, in_specs=in_specs, out_specs=out_specs, check_vma=False)
```

```python
import functools

import jax
import jax.numpy as jnp
from jax import lax
from jax.experimental import pallas as pl
from jax.experimental.pallas import tpu as pltpu
from jax.sharding import PartitionSpec as P

BLOCK = 64
NX = 4
NY = 8
AHEAD = 4
ROWS_A = 64
VMEM_INNER = 16 * 1024 * 1024
VMEM_UPDATE = 24 * 1024 * 1024


def split(value):
    high = value.astype(jnp.bfloat16)
    low = (value - high.astype(jnp.float32)).astype(jnp.bfloat16)
    return high, low


def dot(left, right):
    return jnp.dot(left, right, preferred_element_type=jnp.float32)


def shape_own(drawn, row_index, first_row, row_count):
    panels, rows, width = drawn.shape
    local_rows = first_row + jnp.arange(rows, dtype=jnp.int32)
    matrix_rows = local_rows // BLOCK * BLOCK * row_count + row_index * BLOCK + local_rows % BLOCK
    matrix_rows = matrix_rows[None, :, None]
    diagonal_at = (
        jnp.arange(panels, dtype=jnp.int32)[:, None, None] * width
        + jnp.arange(width, dtype=jnp.int32)[None, None, :]
    )
    shaped = jnp.where(
        matrix_rows < diagonal_at,
        jnp.float32(0.0),
        jnp.where(matrix_rows == diagonal_at, jnp.float32(1.0), drawn),
    )
    return jnp.concatenate([shaped[1], shaped[0]], axis=1)


def move_x(value, shift):
    pairs = [(y * NX + x, y * NX + (x + shift) % NX) for y in range(NY) for x in range(NX)]
    return lax.ppermute(value, "col", pairs)


def move_y(value, shift):
    pairs = [(y * NX + x, (y + shift) % NY * NX + x) for y in range(NY) for x in range(NX)]
    return lax.ppermute(value, "col", pairs)


GROUPS_X = [[y * NX + x for x in range(NX)] for y in range(NY)]
GROUPS_Y = [[y * NX + x for y in range(NY)] for x in range(NX)]


def spread(value, groups):
    count = len(groups[0])
    copies = jnp.broadcast_to(value[None], (count,) + value.shape)
    return lax.all_to_all(copies, "col", 0, 0, axis_index_groups=groups)


SHIFTS_B = [0, -1, 1, NX // 2]
SHIFTS_A = [0, -1, 1, -2, 2, -3, 3, NY // 2]


def eig_a(y):
    return pl.ds(y, 1), pl.ds(0, NX), pl.ds(0, ROWS_A)


def eig_b(x, rows):
    return pl.ds(0, NY), pl.ds(x, 1), pl.ds(ROWS_A, rows - ROWS_A)


def pieces_of(at_ref, shifts, rows):
    places = [eig_b(at_ref[SHIFTS_B.index(shift)], rows) for shift in shifts[0]]
    return places + [eig_a(at_ref[NX + SHIFTS_A.index(shift)]) for shift in shifts[1]]


def load(source, target, sem):
    copy = pltpu.make_async_copy(source, target, sem)
    copy.start()
    return copy


def add_products(inner_ref, gram_ref, eig, panel):
    cols = eig.shape[1]
    width = panel.shape[1] // 2
    high, low = split(eig.T)
    parts = jnp.concatenate([high, low], axis=0)
    panel_high, panel_low = split(panel)
    both = dot(parts, panel_high)
    inner_ref[...] += both[:cols] + (both[cols:] + dot(high, panel_low))
    high = panel_high[:, width:].T
    low = panel_low[:, width:].T
    gram_ref[...] += dot(high, panel_high[:, :width]) + (
        dot(low, panel_high[:, :width]) + dot(high, panel_low[:, :width])
    )


def whole(value):
    return pl.BlockSpec(value.shape, lambda i, at_ref: (0,) * len(value.shape))


def inner_kernel(shifts, first, last, at_ref, eig_ref, *refs):
    count = len(shifts[0]) + len(shifts[1])
    panels, refs = refs[:count], refs[count:]
    if first:
        starts = None
    else:
        starts, refs = refs[:2], refs[2:]
    outs, (inner_ref, gram_ref) = refs[:-2], refs[-2:]
    inner_ref[...] = jnp.zeros_like(inner_ref) if first else starts[0][...]
    gram_ref[...] = jnp.zeros_like(gram_ref) if first else starts[1][...]
    for panel_ref, where in zip(panels, pieces_of(at_ref, shifts, eig_ref.shape[2])):
        eig = eig_ref[where]
        add_products(inner_ref, gram_ref, eig.reshape(-1, eig.shape[-1]), panel_ref[...])
    if not last:
        outs[0][...] = inner_ref[...]
        outs[1][...] = gram_ref[...]
        return
    (out_ref,) = outs
    shares, share, width = out_ref.shape
    half = gram_ref.shape[0] // 2
    out_ref[:, : share // 2, :] = inner_ref[...].reshape(shares, share // 2, width)
    gram = jnp.concatenate([gram_ref[:half, :], gram_ref[half:, :]], axis=1)
    out_ref[:, share // 2 :, :] = gram.reshape(shares, share // 2, width)


def inner_products(at, eigs, shifts, panels, starts, shares):
    cols = eigs.shape[3]
    width = panels[0].shape[1]
    total = sum(panel.shape[0] for panel in panels)
    state = [jax.ShapeDtypeStruct(shape, jnp.float32) for shape in [(cols, width), (width // 2, width // 2)]]
    outs = [jax.ShapeDtypeStruct((shares, 2 * cols // shares, width), jnp.float32)] if shares else state
    args = [eigs, *panels] + ([] if starts is None else list(starts))
    return pl.pallas_call(
        functools.partial(inner_kernel, shifts, starts is None, bool(shares)),
        grid_spec=pltpu.PrefetchScalarGridSpec(
            num_scalar_prefetch=1,
            grid=(1,),
            in_specs=[whole(arg) for arg in args],
            out_specs=[whole(out) for out in outs],
            scratch_shapes=[pltpu.VMEM(shape.shape, jnp.float32) for shape in state],
        ),
        out_shape=outs,
        compiler_params=pltpu.CompilerParams(vmem_limit_bytes=VMEM_INNER),
        cost_estimate=pl.CostEstimate(
            flops=12 * total * cols * width, bytes_accessed=4 * total * (width + cols), transcendentals=0
        ),
    )(at, *args)


def times(left, right):
    def part(one, other):
        return lax.dot_general(one, other, (((1,), (1,)), ((), ())), preferred_element_type=jnp.float32)

    (left_high, left_low), (high, low) = split(left), split(right)
    return part(left_high, high) + (part(left_high, low) + part(left_low, high))


def triangle(tau):
    row = lax.broadcasted_iota(jnp.int32, tau.shape, 0)
    col = lax.broadcasted_iota(jnp.int32, tau.shape, 1)
    return jnp.where(row < col, tau, jnp.where(row == col, jnp.float32(1.0), jnp.float32(0.0)))


def update_kernel(at_ref, sums_ref, tau_hbm, eig_hbm, *refs):
    panels, out_ref = refs[: NX + NY], refs[NX + NY]
    parts_ref, tau_ref, eig_ref, buf_ref, own_sems, sems, out_sems = refs[NX + NY + 1 :]
    rows, cols = eig_ref.shape[2:]
    width = tau_ref.shape[1]
    tau_load = load(tau_hbm, tau_ref, own_sems.at[0])
    eig_load = load(eig_hbm, eig_ref, own_sems.at[1])
    spans = [0]
    for panel_ref in panels:
        spans.append(spans[-1] + panel_ref.shape[0])

    def start(n):
        return load(panels[n], buf_ref.at[pl.ds(spans[n], panels[n].shape[0])], sems.at[n])

    copies = [start(n) for n in range(AHEAD)]
    tau_load.wait()
    own_cols = sums_ref.shape[1] // 2
    inner = sums_ref[:, :own_cols, :].reshape(cols, 2 * width)
    gram = sums_ref[:, own_cols:, :].reshape(cols, 2 * width)
    gram = jnp.concatenate([gram[:, :width], gram[:, width:]], axis=0)
    s_two = times(inner[:, :width], triangle(tau_ref[1]))
    s_one = times(inner[:, width:] - times(s_two, gram), triangle(tau_ref[0]))
    high, low = split(jnp.concatenate([s_two, s_one], axis=1).T)
    parts_ref[:, :cols] = high
    parts_ref[:, cols:] = low

    eig_load.wait()
    stores = []
    for n, where in enumerate(pieces_of(at_ref, (SHIFTS_B, SHIFTS_A), rows)):
        copies[n].wait()
        if n + AHEAD < len(panels):
            copies.append(start(n + AHEAD))
        high, low = split(buf_ref[spans[n] : spans[n + 1], :])
        both = dot(high, parts_ref[...])
        change = both[:, :cols] + (both[:, cols:] + dot(low, parts_ref[:, :cols]))
        old = eig_ref[where]
        eig_ref[where] = old - change.reshape(old.shape)
        if n >= NX:
            stores.append(load(eig_ref.at[where[0]], out_ref.at[where[0]], out_sems.at[n - NX]))
    for copy in stores:
        copy.wait()


def in_hbm(value):
    return pltpu.with_memory_space_constraint(value, pltpu.HBM)


def update(at, eigs, sums, tau, panels):
    cols = eigs.shape[3]
    width = panels[0].shape[1]
    total = sum(panel.shape[0] for panel in panels)
    anywhere = pl.BlockSpec(memory_space=pl.ANY)
    return pl.pallas_call(
        update_kernel,
        grid_spec=pltpu.PrefetchScalarGridSpec(
            num_scalar_prefetch=1,
            grid=(1,),
            in_specs=[whole(sums)] + [anywhere] * (2 + len(panels)),
            out_specs=anywhere,
            scratch_shapes=[
                pltpu.VMEM((width, 2 * cols), jnp.bfloat16),
                pltpu.VMEM(tau.shape, jnp.float32),
                pltpu.VMEM(eigs.shape, jnp.float32),
                pltpu.VMEM((total, width), jnp.float32),
                pltpu.SemaphoreType.DMA((2,)),
                pltpu.SemaphoreType.DMA((NX + NY,)),
                pltpu.SemaphoreType.DMA((NY,)),
            ],
        ),
        out_shape=jax.ShapeDtypeStruct(eigs.shape, jnp.float32),
        compiler_params=pltpu.CompilerParams(vmem_limit_bytes=VMEM_UPDATE),
        cost_estimate=pl.CostEstimate(
            flops=6 * total * cols * width, bytes_accessed=4 * total * (width + 2 * cols), transcendentals=0
        ),
    )(at, sums, in_hbm(tau), in_hbm(eigs), *[in_hbm(panel) for panel in panels])


def shards(eigvecs, reflectors, tau_blocks):
    row_index = lax.axis_index("row")
    col_index = lax.axis_index("col")
    row_count = lax.axis_size("row")
    width = 2 * tau_blocks.shape[1]
    y_at, x_at = (col_index // NX).astype(jnp.int32), (col_index % NX).astype(jnp.int32)
    at = jnp.concatenate(
        [(x_at + NX + jnp.array(SHIFTS_B, jnp.int32)) % NX, (y_at + NY + jnp.array(SHIFTS_A, jnp.int32)) % NY]
    )
    eigs = eigvecs.reshape(NY, NX, reflectors.shape[1], eigvecs.shape[1])

    first_row = col_index * reflectors.shape[1]
    rest = shape_own(reflectors[:, ROWS_A:], row_index, first_row + ROWS_A, row_count)
    own = shape_own(reflectors[:, :ROWS_A], row_index, first_row, row_count)

    own_a = lax.all_gather(own, "col", axis=0, tiled=True, axis_index_groups=GROUPS_X)
    own_b = spread(rest, GROUPS_Y).reshape(-1, width)
    own_b, _ = lax.optimization_barrier((own_b, own_a))
    up, down = [own_a], [own_a]
    for _ in range(NY // 2 - 1):
        up.append(move_y(up[-1], 1))
        down.append(move_y(down[-1], -1))
    far_a = move_y(up[-1], 1)
    left, right = move_x(own_b, 1), move_x(own_b, -1)
    far_b = move_x(left, 1)

    state = inner_products(at, eigs, ([0], [0, -1, 1]), [own_b, own_a, up[1], down[1]], None, 0)
    state = inner_products(at, eigs, ([-1, 1], [-2, 2]), [left, right, up[2], down[2]], state, 0)
    (shares,) = inner_products(
        at, eigs, ([NX // 2], [-3, 3, NY // 2]), [far_b, up[3], down[3], far_a], state, row_count
    )
    share = jnp.sum(lax.all_to_all(shares, "row", 0, 0), axis=0)
    sums = lax.all_gather(share, "row")

    panels = [own_b, left, right, far_b, own_a, up[1], down[1], up[2], down[2], up[3], down[3], far_a]
    return update(at, eigs, sums, tau_blocks, panels).reshape(eigvecs.shape)


def solution(mesh):
    in_specs = (P("row", "col"), P(None, ("row", "col"), None), P())
    out_specs = P("row", "col")
    return jax.shard_map(shards, mesh=mesh, in_specs=in_specs, out_specs=out_specs, check_vma=False)
```

```python
import functools

import jax
import jax.numpy as jnp
from jax import lax
from jax.experimental import pallas as pl
from jax.experimental.pallas import tpu as pltpu
from jax.sharding import PartitionSpec as P

BLOCK = 64
NX = 4
NY = 8
AHEAD = 4
ROWS_A = 64
VMEM_INNER = 16 * 1024 * 1024
VMEM_UPDATE = 24 * 1024 * 1024


def split(value):
    high = value.astype(jnp.bfloat16)
    low = (value - high.astype(jnp.float32)).astype(jnp.bfloat16)
    return high, low


def dot(left, right):
    return jnp.dot(left, right, preferred_element_type=jnp.float32)


def shape_own(drawn, row_index, first_row, row_count):
    panels, rows, width = drawn.shape
    local_rows = first_row + jnp.arange(rows, dtype=jnp.int32)
    matrix_rows = local_rows // BLOCK * BLOCK * row_count + row_index * BLOCK + local_rows % BLOCK
    matrix_rows = matrix_rows[None, :, None]
    diagonal_at = (
        jnp.arange(panels, dtype=jnp.int32)[:, None, None] * width
        + jnp.arange(width, dtype=jnp.int32)[None, None, :]
    )
    shaped = jnp.where(
        matrix_rows < diagonal_at,
        jnp.float32(0.0),
        jnp.where(matrix_rows == diagonal_at, jnp.float32(1.0), drawn),
    )
    return jnp.concatenate([shaped[1], shaped[0]], axis=1)


def move_x(value, shift):
    pairs = [(y * NX + x, y * NX + (x + shift) % NX) for y in range(NY) for x in range(NX)]
    return lax.ppermute(value, "col", pairs)


def move_y(value, shift):
    pairs = [(y * NX + x, (y + shift) % NY * NX + x) for y in range(NY) for x in range(NX)]
    return lax.ppermute(value, "col", pairs)


GROUPS_X = [[y * NX + x for x in range(NX)] for y in range(NY)]
GROUPS_Y = [[y * NX + x for y in range(NY)] for x in range(NX)]


def spread(value, groups):
    count = len(groups[0])
    copies = jnp.broadcast_to(value[None], (count,) + value.shape)
    return lax.all_to_all(copies, "col", 0, 0, axis_index_groups=groups)


SHIFTS_B = [0, -1, 1, NX // 2]
SHIFTS_A = [0, -1, 1, -2, 2, -3, 3, NY // 2]


def eig_a(y):
    return pl.ds(y, 1), pl.ds(0, NX), pl.ds(0, ROWS_A)


def eig_b(x, rows):
    return pl.ds(0, NY), pl.ds(x, 1), pl.ds(ROWS_A, rows - ROWS_A)


def pieces_of(at_ref, shifts, rows):
    places = [eig_b(at_ref[SHIFTS_B.index(shift)], rows) for shift in shifts[0]]
    return places + [eig_a(at_ref[NX + SHIFTS_A.index(shift)]) for shift in shifts[1]]


def load(source, target, sem):
    copy = pltpu.make_async_copy(source, target, sem)
    copy.start()
    return copy


def add_products(inner_ref, gram_ref, eig, panel):
    cols = eig.shape[1]
    width = panel.shape[1] // 2
    high, low = split(eig.T)
    parts = jnp.concatenate([high, low], axis=0)
    panel_high, panel_low = split(panel)
    both = dot(parts, panel_high)
    inner_ref[...] += both[:cols] + (both[cols:] + dot(high, panel_low))
    high = panel_high[:, width:].T
    low = panel_low[:, width:].T
    gram_ref[...] += dot(high, panel_high[:, :width]) + (
        dot(low, panel_high[:, :width]) + dot(high, panel_low[:, :width])
    )


def whole(value):
    return pl.BlockSpec(value.shape, lambda i, at_ref: (0,) * len(value.shape))


def inner_kernel(shifts, first, last, at_ref, eig_ref, *refs):
    count = len(shifts[0]) + len(shifts[1])
    panels, refs = refs[:count], refs[count:]
    if first:
        starts = None
    else:
        starts, refs = refs[:2], refs[2:]
    outs, (inner_ref, gram_ref) = refs[:-2], refs[-2:]
    inner_ref[...] = jnp.zeros_like(inner_ref) if first else starts[0][...]
    gram_ref[...] = jnp.zeros_like(gram_ref) if first else starts[1][...]
    for panel_ref, where in zip(panels, pieces_of(at_ref, shifts, eig_ref.shape[2])):
        eig = eig_ref[where]
        add_products(inner_ref, gram_ref, eig.reshape(-1, eig.shape[-1]), panel_ref[...])
    if not last:
        outs[0][...] = inner_ref[...]
        outs[1][...] = gram_ref[...]
        return
    (out_ref,) = outs
    shares, share, width = out_ref.shape
    half = gram_ref.shape[0] // 2
    out_ref[:, : share // 2, :] = inner_ref[...].reshape(shares, share // 2, width)
    gram = jnp.concatenate([gram_ref[:half, :], gram_ref[half:, :]], axis=1)
    out_ref[:, share // 2 :, :] = gram.reshape(shares, share // 2, width)


def inner_products(at, eigs, shifts, panels, starts, shares):
    cols = eigs.shape[3]
    width = panels[0].shape[1]
    total = sum(panel.shape[0] for panel in panels)
    state = [jax.ShapeDtypeStruct(shape, jnp.float32) for shape in [(cols, width), (width // 2, width // 2)]]
    outs = [jax.ShapeDtypeStruct((shares, 2 * cols // shares, width), jnp.float32)] if shares else state
    args = [eigs, *panels] + ([] if starts is None else list(starts))
    return pl.pallas_call(
        functools.partial(inner_kernel, shifts, starts is None, bool(shares)),
        grid_spec=pltpu.PrefetchScalarGridSpec(
            num_scalar_prefetch=1,
            grid=(1,),
            in_specs=[whole(arg) for arg in args],
            out_specs=[whole(out) for out in outs],
            scratch_shapes=[pltpu.VMEM(shape.shape, jnp.float32) for shape in state],
        ),
        out_shape=outs,
        compiler_params=pltpu.CompilerParams(vmem_limit_bytes=VMEM_INNER),
        cost_estimate=pl.CostEstimate(
            flops=12 * total * cols * width, bytes_accessed=4 * total * (width + cols), transcendentals=0
        ),
    )(at, *args)


def times(left, right):
    def part(one, other):
        return lax.dot_general(one, other, (((1,), (1,)), ((), ())), preferred_element_type=jnp.float32)

    (left_high, left_low), (high, low) = split(left), split(right)
    return part(left_high, high) + (part(left_high, low) + part(left_low, high))


def triangle(tau):
    row = lax.broadcasted_iota(jnp.int32, tau.shape, 0)
    col = lax.broadcasted_iota(jnp.int32, tau.shape, 1)
    return jnp.where(row < col, tau, jnp.where(row == col, jnp.float32(1.0), jnp.float32(0.0)))


def update_kernel(at_ref, sums_ref, tau_hbm, eig_hbm, *refs):
    panels, out_ref = refs[: NX + NY], refs[NX + NY]
    parts_ref, tau_ref, eig_ref, buf_ref, own_sems, sems, out_sems = refs[NX + NY + 1 :]
    rows, cols = eig_ref.shape[2:]
    width = tau_ref.shape[1]
    tau_load = load(tau_hbm, tau_ref, own_sems.at[0])
    eig_load = load(eig_hbm, eig_ref, own_sems.at[1])
    spans = [0]
    for panel_ref in panels:
        spans.append(spans[-1] + panel_ref.shape[0])

    def start(n):
        return load(panels[n], buf_ref.at[pl.ds(spans[n], panels[n].shape[0])], sems.at[n])

    copies = [start(n) for n in range(AHEAD)]
    tau_load.wait()
    own_cols = sums_ref.shape[1] // 2
    inner = sums_ref[:, :own_cols, :].reshape(cols, 2 * width)
    gram = sums_ref[:, own_cols:, :].reshape(cols, 2 * width)
    gram = jnp.concatenate([gram[:, :width], gram[:, width:]], axis=0)
    s_two = times(inner[:, :width], triangle(tau_ref[1]))
    s_one = times(inner[:, width:] - times(s_two, gram), triangle(tau_ref[0]))
    high, low = split(jnp.concatenate([s_two, s_one], axis=1).T)
    parts_ref[:, :cols] = high
    parts_ref[:, cols:] = low

    eig_load.wait()
    stores = []
    for n, where in enumerate(pieces_of(at_ref, (SHIFTS_B, SHIFTS_A), rows)):
        copies[n].wait()
        if n + AHEAD < len(panels):
            copies.append(start(n + AHEAD))
        high, low = split(buf_ref[spans[n] : spans[n + 1], :])
        both = dot(high, parts_ref[...])
        change = both[:, :cols] + (both[:, cols:] + dot(low, parts_ref[:, :cols]))
        old = eig_ref[where]
        eig_ref[where] = old - change.reshape(old.shape)
        if n >= NX:
            stores.append(load(eig_ref.at[where[0]], out_ref.at[where[0]], out_sems.at[n - NX]))
    for copy in stores:
        copy.wait()


def in_hbm(value):
    return pltpu.with_memory_space_constraint(value, pltpu.HBM)


def update(at, eigs, sums, tau, panels):
    cols = eigs.shape[3]
    width = panels[0].shape[1]
    total = sum(panel.shape[0] for panel in panels)
    anywhere = pl.BlockSpec(memory_space=pl.ANY)
    return pl.pallas_call(
        update_kernel,
        grid_spec=pltpu.PrefetchScalarGridSpec(
            num_scalar_prefetch=1,
            grid=(1,),
            in_specs=[whole(sums)] + [anywhere] * (2 + len(panels)),
            out_specs=anywhere,
            scratch_shapes=[
                pltpu.VMEM((width, 2 * cols), jnp.bfloat16),
                pltpu.VMEM(tau.shape, jnp.float32),
                pltpu.VMEM(eigs.shape, jnp.float32),
                pltpu.VMEM((total, width), jnp.float32),
                pltpu.SemaphoreType.DMA((2,)),
                pltpu.SemaphoreType.DMA((NX + NY,)),
                pltpu.SemaphoreType.DMA((NY,)),
            ],
        ),
        out_shape=jax.ShapeDtypeStruct(eigs.shape, jnp.float32),
        compiler_params=pltpu.CompilerParams(vmem_limit_bytes=VMEM_UPDATE),
        cost_estimate=pl.CostEstimate(
            flops=6 * total * cols * width, bytes_accessed=4 * total * (width + 2 * cols), transcendentals=0
        ),
    )(at, sums, in_hbm(tau), in_hbm(eigs), *[in_hbm(panel) for panel in panels])


def shards(eigvecs, reflectors, tau_blocks):
    row_index = lax.axis_index("row")
    col_index = lax.axis_index("col")
    row_count = lax.axis_size("row")
    width = 2 * tau_blocks.shape[1]
    y_at, x_at = (col_index // NX).astype(jnp.int32), (col_index % NX).astype(jnp.int32)
    at = jnp.concatenate(
        [(x_at + NX + jnp.array(SHIFTS_B, jnp.int32)) % NX, (y_at + NY + jnp.array(SHIFTS_A, jnp.int32)) % NY]
    )
    eigs = eigvecs.reshape(NY, NX, reflectors.shape[1], eigvecs.shape[1])

    first_row = col_index * reflectors.shape[1]
    rest = shape_own(reflectors[:, ROWS_A:], row_index, first_row + ROWS_A, row_count)
    own = shape_own(reflectors[:, :ROWS_A], row_index, first_row, row_count)

    own_a = lax.all_gather(own, "col", axis=0, tiled=True, axis_index_groups=GROUPS_X)
    own_b = spread(rest, GROUPS_Y).reshape(-1, width)
    own_b, _ = lax.optimization_barrier((own_b, own_a))
    up, down = [own_a], [own_a]
    for _ in range(NY // 2 - 1):
        up.append(move_y(up[-1], 1))
        down.append(move_y(down[-1], -1))
    far_a = move_y(up[-1], 1)
    left, right = move_x(own_b, 1), move_x(own_b, -1)
    far_b = move_x(left, 1)

    state = inner_products(at, eigs, ([0], [0, -1, 1]), [own_b, own_a, up[1], down[1]], None, 0)
    state = inner_products(
        at, eigs, ([-1, 1], [-2, 2, -3, 3]), [left, right, up[2], down[2], up[3], down[3]], state, 0
    )
    (shares,) = inner_products(at, eigs, ([NX // 2], [NY // 2]), [far_b, far_a], state, row_count)
    share = jnp.sum(lax.all_to_all(shares, "row", 0, 0), axis=0)
    sums = lax.all_gather(share, "row")

    panels = [own_b, left, right, far_b, own_a, up[1], down[1], up[2], down[2], up[3], down[3], far_a]
    return update(at, eigs, sums, tau_blocks, panels).reshape(eigvecs.shape)


def solution(mesh):
    in_specs = (P("row", "col"), P(None, ("row", "col"), None), P())
    out_specs = P("row", "col")
    return jax.shard_map(shards, mesh=mesh, in_specs=in_specs, out_specs=out_specs, check_vma=False)
```
